32 devices in a mesh: dp: 8 (over z, y), seq: 4 (over x, core).
Axes of the slice: x: 2, y: 2, z: 4, core: 2. Of those that a mesh axis runs over, the one named last changes fastest.
Arguments:
- tokens: bfloat16 [8, 4096, 512], P('dp', 'seq'), may hold values from -6 to 6
- in_proj: bfloat16 [512, 1536], replicated, may hold values from -0.25 to 0.25
- out_proj: bfloat16 [512, 512], replicated, may hold values from -3 to 3
- up_proj: bfloat16 [512, 2048], replicated, may hold values from -0.25 to 0.25
- down_proj: bfloat16 [2048, 512], replicated, may hold values from -0.125 to 0.125
- up_bias: bfloat16 [2048], replicated, may hold values from -3 to 3
- down_bias: bfloat16 [512], replicated, may hold values from -2 to 2
- attn_gain: bfloat16 [512], replicated, may hold values from 0.5 to 1.5
- attn_shift: bfloat16 [512], replicated, may hold values from -2 to 2
- ffn_gain: bfloat16 [512], replicated, may hold values from 0.5 to 1.5
- ffn_shift: bfloat16 [512], replicated, may hold values from -2 to 2
- feature_matrix: bfloat16 [8, 64, 256], replicated, may hold values from -5 to 5
- lengths: int32 [8], replicated, may hold values from 1 to 4096, 16384 in all
- slot_of_seq: int32 [8], replicated, may hold values from 0 to 7, each once
- cotangent: bfloat16 [8, 4096, 512], P('dp', 'seq'), may hold values from -6 to 6
Outputs:
- layer_out: bfloat16 [8, 4096, 512], P('dp', 'seq')
- grad_tokens: bfloat16 [8, 4096, 512], P('dp', 'seq')
- grad_in_proj: float32 [512, 1536], replicated
- grad_out_proj: float32 [512, 512], replicated
- grad_up_proj: float32 [512, 2048], replicated
- grad_down_proj: float32 [2048, 512], replicated
- grad_up_bias: float32 [2048], replicated
- grad_down_bias: float32 [512], replicated
- grad_attn_gain: float32 [512], replicated
- grad_attn_shift: float32 [512], replicated
- grad_ffn_gain: float32 [512], replicated
- grad_ffn_shift: float32 [512], replicated
The draws below stay inside these ranges and needn't reach their ends.
Inputs may be any that keep to these rules, and one draw needn't show every extreme that they name: The lengths sum to 16384 and the longest is exactly 4096. `slot_of_seq`: each slot holds exactly one sequence.
All inputs are finite; a program needn't handle non-finite values.
Results may differ from the reference program's by a relative error of at most 0.02.
Values sent between devices are 32-bit elements; how exact they have to be, the bound alone decides.
No kernel may reach another device: no remote copies, remote signals or barrier semaphores. Data moves between devices by JAX's collectives and lax.ppermute only.
A program may use at most 256 MiB of HBM per device.

```python
import math
import jax
import jax.numpy as jnp
import numpy as np
from jax import lax

D = 512
HEADS = 8
HEAD_DIM = 64
FEATS = 256
FF = 2048
BLOCK = 512
LEN = 4096
SEQS = 8


def level_of(rng, dims, cuts, low, largest):
    def one(dim, blocks):
        steps = jax.random.uniform(jax.random.fold_in(jax.random.fold_in(rng, 6), dim), (blocks,), jnp.float32, low / len(cuts), largest / len(cuts))
        return jnp.repeat(jnp.exp(steps), dims[dim] // blocks).reshape((-1,) + (1,) * (len(dims) - dim - 1))

    level = one(*cuts[0])
    for cut in cuts[1:]:
        level = level * one(*cut)
    return level


def profile(amount, total, limit, slope):
    weights = [(1 << 20) // math.isqrt(rank ** slope) + 1 for rank in range(2, amount + 1)]
    spare, counts = total - limit - (amount - 1), [1] * (amount - 1)
    while spare > 0:
        free = [i for i in range(amount - 1) if counts[i] < limit]
        mass, remaining = sum([weights[i] for i in free]), spare
        for i in free:
            more = min(limit - counts[i], max(1, remaining * weights[i] // mass), spare)
            counts[i] = counts[i] + more
            spare = spare - more
    return np.array([limit] + counts)


def uneven(key, number_of, total, most, lean):
    if number_of == 2:
        one = jax.random.randint(key, (), max(1, total - most), min(most, total - 1) + 1)
        return jnp.stack([one, total - one])
    tallies = jnp.asarray(profile(number_of, total, most, lean), jnp.int32)
    twos = (number_of - 1) // 2
    source_of, taker = tallies[1:1 + 2 * twos:2], tallies[2:2 + 2 * twos:2]
    margin = jnp.minimum(source_of - 1, most - taker)
    passed = jax.random.randint(jax.random.fold_in(key, 1), (twos,), 0, 1 << 20) % (margin + 1)
    tallies = tallies.at[1:1 + 2 * twos:2].set(source_of - passed).at[2:2 + 2 * twos:2].set(taker + passed)
    return tallies[jax.random.permutation(jax.random.fold_in(key, 2), number_of)]


def scatter_about(own_key, dims, spread, bound, cuts=(), kind=jnp.bfloat16):
    entries = spread * jax.random.normal(own_key, dims, jnp.float32)
    if cuts:
        entries = entries * level_of(own_key, dims, cuts, -0.22, 0.18)
    return jnp.clip(entries, -bound, bound).astype(kind)


def setup_inputs(seed: int = 0) -> dict:
    keys = jax.random.split(jax.random.key(seed), 16)
    tokens = scatter_about(keys[0], (SEQS, LEN, D), 1.0, 6.0, ((0, 8), (1, 4)))
    in_proj = scatter_about(keys[1], (D, 3 * D), D ** -0.5, 0.25)
    out_proj = scatter_about(keys[2], (D, D), (max(1, D // 128)) ** -0.5, 3.0)
    up_proj = scatter_about(keys[3], (D, FF), D ** -0.5, 0.25)
    down_proj = scatter_about(keys[4], (FF, D), FF ** -0.5, 0.125)
    up_bias = scatter_about(keys[5], (FF,), 0.5, 3.0)
    down_bias = scatter_about(keys[6], (D,), 0.3, 2.0)
    attn_gain = jnp.clip(1.0 + 0.1 * jax.random.normal(keys[7], (D,), jnp.float32), 0.5, 1.5).astype(jnp.bfloat16)
    attn_shift = scatter_about(keys[8], (D,), 0.3, 2.0)
    ffn_gain = jnp.clip(1.0 + 0.1 * jax.random.normal(keys[9], (D,), jnp.float32), 0.5, 1.5).astype(jnp.bfloat16)
    ffn_shift = scatter_about(keys[10], (D,), 0.3, 2.0)
    feature_matrix = scatter_about(keys[11], (HEADS, HEAD_DIM, FEATS), 1.0, 5.0)
    lengths = uneven(keys[12], SEQS, SEQS * LEN // 2, LEN, 2).astype(jnp.int32)
    slot_of_seq = jax.random.permutation(keys[13], SEQS).astype(jnp.int32)
    cotangent = scatter_about(keys[14], (SEQS, LEN, D), 1.0, 6.0, ((0, 8), (1, 4)))
    return {"tokens": tokens, "in_proj": in_proj, "out_proj": out_proj, "up_proj": up_proj, "down_proj": down_proj, "up_bias": up_bias, "down_bias": down_bias, "attn_gain": attn_gain, "attn_shift": attn_shift, "ffn_gain": ffn_gain, "ffn_shift": ffn_shift, "feature_matrix": feature_matrix, "lengths": lengths, "slot_of_seq": slot_of_seq, "cotangent": cotangent}


norm_eps = 1e-05
highest = lax.Precision.HIGHEST

@jax.custom_vjp
def low(v):
    return lax.optimization_barrier(v.astype(jnp.bfloat16)).astype(jnp.float32)

@jax.custom_vjp
def low_back(v):
    return v

def low_keep(v):
    return (low(v), None)

def low_pass(kept, grad):
    return (grad,)

def back_keep(v):
    return (v, None)

def back_low(kept, grad):
    return (low(grad),)
low.defvjp(low_keep, low_pass)
low_back.defvjp(back_keep, back_low)

def norm_rows(values, norm_gain, norm_shift):
    center = values - lax.optimization_barrier(jnp.mean(values, -1, keepdims=True))
    return center * lax.rsqrt(lax.optimization_barrier(jnp.mean(center * center, -1, keepdims=True)) + norm_eps) * norm_gain + norm_shift

def favor_features(values, feature_matrix):
    factor = values.shape[-1] ** (-0.25)
    raw_proj = low_back(jnp.einsum('lhe,hem->lhm', values, feature_matrix, precision=highest))
    feat_vals = jnp.exp(factor * raw_proj - 0.5 * factor * factor * lax.optimization_barrier(jnp.sum(values * values, -1, keepdims=True))) / math.sqrt(feature_matrix.shape[-1])
    return low(low_back(feat_vals))

def attend_block(carry, pieces):
    state_sum, total_sum = carry
    query_feat, key_feat, value_rows = pieces
    block_rows = query_feat.shape[0]
    causal = (jnp.arange(block_rows, dtype=jnp.int32)[:, None] >= jnp.arange(block_rows, dtype=jnp.int32)[None, :]).astype(jnp.float32)
    scores = low(low_back(jnp.einsum('qhm,khm->hqk', query_feat, key_feat, precision=highest) * causal[None]))
    numerator = low_back(jnp.einsum('hqk,khe->qhe', scores, value_rows, precision=highest) + jnp.einsum('qhm,hme->qhe', query_feat, low(state_sum), precision=highest))
    denominator = low_back(lax.optimization_barrier(jnp.sum(scores, -1)).T + jnp.einsum('qhm,hm->qh', query_feat, low(total_sum), precision=highest))
    mixed_rows = numerator / denominator[..., None]
    state_add = low_back(jnp.einsum('khm,khe->hme', key_feat, value_rows, precision=highest))
    total_add = low_back(lax.optimization_barrier(jnp.sum(key_feat, 0)))
    return ((state_sum + state_add, total_sum + total_add), mixed_rows)

def layer_forward(inputs, in_proj, out_proj, up_proj, down_proj, up_bias, down_bias, attn_gain, attn_shift, ffn_gain, ffn_shift, feature_matrix, keep_rows):
    seq_rows, model_width = inputs.shape
    head_count, head_size, feat_count = feature_matrix.shape
    attn_in = low(norm_rows(inputs, attn_gain, attn_shift))
    projected = low(low_back(jnp.dot(attn_in, in_proj, precision=highest))).reshape(seq_rows, 3, head_count, head_size)
    query_feat = favor_features(projected[:, 0], feature_matrix)
    key_feat = favor_features(projected[:, 1], feature_matrix) * keep_rows[:, None, None]
    block_count = seq_rows // BLOCK
    pieces = (query_feat.reshape(block_count, BLOCK, head_count, feat_count), key_feat.reshape(block_count, BLOCK, head_count, feat_count), projected[:, 2].reshape(block_count, BLOCK, head_count, head_size))
    start_pair = (jnp.zeros((head_count, feat_count, head_size), jnp.float32), jnp.zeros((head_count, feat_count), jnp.float32))
    _, mixed_rows = lax.scan(jax.checkpoint(attend_block), start_pair, pieces)
    mixed_rows = low(mixed_rows.reshape(seq_rows, model_width))
    attn_out = low_back(jnp.dot(mixed_rows, out_proj, precision=highest))
    residual = inputs + keep_rows[:, None] * attn_out
    ffn_in = low(norm_rows(residual, ffn_gain, ffn_shift))
    hidden = low_back(jnp.dot(ffn_in, up_proj, precision=highest) + up_bias)
    activation = low(jax.nn.gelu(hidden, approximate=True))
    ffn_out = low_back(jnp.dot(activation, down_proj, precision=highest) + down_bias)
    return residual + keep_rows[:, None] * ffn_out

def reference(tokens, in_proj, out_proj, up_proj, down_proj, up_bias, down_bias, attn_gain, attn_shift, ffn_gain, ffn_shift, feature_matrix, lengths, slot_of_seq, cotangent):
    owners = (slot_of_seq[:, None] == jnp.arange(SEQS, dtype=jnp.int32)[None, :]).astype(jnp.int32)
    slot_len = lax.optimization_barrier(jnp.sum(lengths[:, None] * owners, 0))
    positions = jnp.arange(LEN, dtype=jnp.int32)
    params = tuple((piece.astype(jnp.float32) for piece in (in_proj, out_proj, up_proj, down_proj, up_bias, down_bias, attn_gain, attn_shift, ffn_gain, ffn_shift)))
    features_wide = feature_matrix.astype(jnp.float32)

    def per_sequence(totals, seq_item):
        seq_tokens, seq_grad, seq_len = seq_item
        keep_rows = (positions < seq_len).astype(jnp.float32)

        def forward(inputs, *weights):
            return layer_forward(inputs, *weights, features_wide, keep_rows)
        outputs, pull = jax.vjp(forward, seq_tokens.astype(jnp.float32), *params)
        grads = pull(seq_grad.astype(jnp.float32))
        totals = tuple((left + right for left, right in zip(totals, grads[1:])))
        return (totals, (outputs.astype(jnp.bfloat16), grads[0].astype(jnp.bfloat16)))
    start = tuple((jnp.zeros(piece.shape, jnp.float32) for piece in params))
    totals, (layer_out, grad_tokens) = lax.scan(per_sequence, start, (tokens, cotangent, slot_len))
    return (layer_out, grad_tokens, totals[0], totals[1], totals[2], totals[3], totals[4], totals[5], totals[6], totals[7], totals[8], totals[9])
```

```python
import jax
import jax.numpy as jnp
from jax import lax
from jax.experimental import pallas as pl
from jax.experimental.pallas import tpu as pltpu
from jax.sharding import PartitionSpec as P

norm_eps = 1e-05
f32 = jnp.float32
bf16 = jnp.bfloat16
BLOCK = 512
TILE = 256
LANES = 128
SROWS = 72
AXES = ("dp", "seq")
gelu_a = 0.7978845608028654
gelu_b = 0.044715


def nn(a, b):
    return lax.dot_general(a, b, (((1,), (0,)), ((), ())), preferred_element_type=f32)


def nt(a, b):
    return lax.dot_general(a, b, (((1,), (1,)), ((), ())), preferred_element_type=f32)


def tn(a, b):
    return lax.dot_general(a, b, (((0,), (0,)), ((), ())), preferred_element_type=f32)


def standardize(values):
    center = values - jnp.mean(values, -1, keepdims=True)
    inverse = lax.rsqrt(jnp.mean(center * center, -1, keepdims=True) + norm_eps)
    return center * inverse, inverse


def norm_back(incoming, scaled, inverse, gain):
    weighted = incoming * gain
    return inverse * (
        weighted
        - jnp.mean(weighted, -1, keepdims=True)
        - scaled * jnp.mean(weighted * scaled, -1, keepdims=True)
    )


def keep_column(sc, start, rows):
    return ((sc[0] + start + lax.broadcasted_iota(jnp.int32, (rows, 1), 0)) < sc[1]).astype(f32)


def lane_ids(rows):
    return lax.broadcasted_iota(jnp.int32, (rows, LANES), 1)


def pair_features(pair, fo):
    wide = pair.astype(f32)
    square = wide * wide
    high = square.astype(bf16)
    low = (square - high.astype(f32)).astype(bf16)
    raw = nn(pair, fo[:LANES])
    total = nn(high, fo[LANES:]) + nn(low, fo[LANES:])
    factor = 64 ** (-0.25)
    return jnp.exp(factor * raw - (0.5 * factor * factor) * total) * (1.0 / 16.0)


def pair_back(rawg, pair, fo):
    factor = 64 ** (-0.25)
    both = nt(rawg, fo)
    return both[:, :LANES] - factor * pair.astype(f32) * both[:, LANES:]


def split_pair(pair, mark):
    lanes = lane_ids(pair.shape[0])
    tail = jnp.where(lanes == 64, mark, 0.0)
    return (
        jnp.where(lanes < 64, pair, tail),
        jnp.where(lanes < 64, pltpu.roll(pair, 64, 1), tail),
    )


def join_pair(one, two):
    return jnp.where(lane_ids(one.shape[0]) < 64, one, pltpu.roll(two, 64, 1))


def key_kernel(sc, tok, wkv, gain, shift, fo, attn_o, k_o, vx_o, kf_o, st_o):
    rows = tok.shape[0]
    scaled, _ = standardize(tok[...].astype(f32))
    attn_in = (scaled * gain[...] + shift[...]).astype(bf16)
    attn_o[...] = attn_in
    keep = keep_column(sc, pl.program_id(0) * rows, rows)
    width = k_o.shape[1]
    for p in range(width // LANES):
        kp = nn(attn_in, wkv[:, p * LANES : (p + 1) * LANES]).astype(bf16)
        k_o[:, p * LANES : (p + 1) * LANES] = kp
        kf_o[:, p * 512 : (p + 1) * 512] = (pair_features(kp, fo[p]) * keep).astype(bf16)
        vp = nn(attn_in, wkv[:, width + p * LANES : width + (p + 1) * LANES])
        one, two = split_pair(vp, 1.0)
        vx_o[:, 2 * p * LANES : (2 * p + 1) * LANES] = one.astype(bf16)
        vx_o[:, (2 * p + 1) * LANES : (2 * p + 2) * LANES] = two.astype(bf16)
        for h in (2 * p, 2 * p + 1):
            part = tn(vx_o[:, h * LANES : (h + 1) * LANES], kf_o[:, h * TILE : (h + 1) * TILE])
            st_o[0, h] = part[:SROWS]


def causal_mask(rows, columns):
    return lax.broadcasted_iota(jnp.int32, (rows, columns), 0), lax.broadcasted_iota(
        jnp.int32, (rows, columns), 1
    )


def near_kernel(attn, wq, fo, kf, vx, q_o, qf_o, near_o):
    rows = attn.shape[0]
    qp = nn(attn[...], wq[...]).astype(bf16)
    q_o[...] = qp
    qf_o[...] = pair_features(qp, fo[0]).astype(bf16)
    for h in range(2):
        fl = slice(h * TILE, (h + 1) * TILE)
        vl = slice(h * LANES, (h + 1) * LANES)
        for base in range(0, rows, BLOCK):
            for t in range(base, base + BLOCK, TILE):
                span = t + TILE - base
                scores = nt(qf_o[t : t + TILE, fl], kf[base : base + span, fl])
                row, column = causal_mask(TILE, span)
                scores = jnp.where(row + (t - base) >= column, scores, 0.0).astype(bf16)
                near_o[t : t + TILE, vl] = nn(scores, vx[base : base + span, vl])


def mix_kernel(sc, near, qf, pre, st, tok, wout, gain, shift, num_o, mix_o, low_o, res_o, fin_o):
    i = pl.program_id(0)
    rows = near.shape[0]
    heads = pre.shape[0]
    pad = jnp.zeros((LANES - SROWS, TILE), f32)
    for h in range(heads):
        state = pre[h]
        for b in range(st.shape[0] - 1):
            state = state + jnp.where(b < i, st[b, h], 0.0)
        low = jnp.concatenate([state, pad], 0).astype(bf16)
        low_o[0, h] = low
        hl = slice(h * LANES, (h + 1) * LANES)
        num = near[:, hl] + nt(qf[:, h * TILE : (h + 1) * TILE], low)
        num_o[:, hl] = num
        mix_o[:, hl] = (num / num[:, 64:65]).astype(bf16)
    attn_out = nn(mix_o[...], wout[...])
    residual = tok[...].astype(f32) + keep_column(sc, i * rows, rows) * attn_out
    res_o[...] = residual
    scaled, _ = standardize(residual)
    fin_o[...] = (scaled * gain[...] + shift[...]).astype(bf16)


def ffn_body(sc, fin, cot, up, down, ub, fo_prev, fig_prev, keep_o, send_o, fo_o, fig_o, ubg_o, fg_s, act_s, hg_s):
    j = pl.program_id(0)
    rows = fin.shape[0]
    chunk = up.shape[1]
    half = fin.shape[1] // 2

    @pl.when(j == 0)
    def _():
        fg_s[...] = (keep_column(sc, 0, rows) * cot[...].astype(f32)).astype(bf16)

    bias = ub[...]
    sums = jnp.zeros((1, chunk), f32)
    for t in range(0, rows, TILE):
        rl = slice(t, t + TILE)
        x = nn(fin[rl], up[...]) + bias
        x2 = x * x
        th = jnp.tanh(gelu_a * (x + gelu_b * (x2 * x)))
        half_one = 0.5 * (1.0 + th)
        act = (x * half_one).astype(bf16)
        act_s[rl] = act
        slope = half_one + (0.5 * x) * (1.0 - th * th) * (gelu_a + (3.0 * gelu_a * gelu_b) * x2)
        hg = (nt(fg_s[rl], down[...]) * slope).astype(bf16)
        hg_s[rl] = hg
        sums = sums + jnp.sum(hg.astype(f32), 0, keepdims=True)
        out = nn(act, down[...])
        back = nt(hg, up[...])

        @pl.when(j == 0)
        def _():
            if fo_prev is None:
                fo_o[rl] = out
                fig_o[rl] = back
            else:
                fo_o[rl] = fo_prev[rl] + out
                fig_o[rl] = fig_prev[rl] + back

        @pl.when(j > 0)
        def _():
            fo_o[rl] = fo_o[rl] + out
            fig_o[rl] = fig_o[rl] + back

    ubg_o[...] = sums
    mine = pl.multiple_of(sc[2] * half, half)
    other = pl.multiple_of((1 - sc[2]) * half, half)
    span = 2 * chunk
    for ref, first in ((send_o, other), (keep_o, mine)):
        ref[:, pl.ds(pl.multiple_of(j * chunk, chunk), chunk)] = tn(fin[:, pl.ds(first, half)], hg_s[...])
        ref[:, pl.ds(pl.multiple_of(span + j * chunk, chunk), chunk)] = tn(
            act_s[:, pl.ds(first, half)], fg_s[...]
        )


def ffn_first(sc, fin, cot, up, down, ub, *rest):
    ffn_body(sc, fin, cot, up, down, ub, None, None, *rest)


def ffn_second(sc, fin, cot, up, down, ub, fo_prev, fig_prev, *rest):
    ffn_body(sc, fin, cot, up, down, ub, fo_prev, fig_prev, *rest)


def middle_kernel(sc, fo, fig, res, cot, mix, num, qf, wout, gain, dbias,
                  lay_o, rg_o, ngx_o, gst_o, og_o, small_o):
    i = pl.program_id(0)
    rows = fo.shape[0]
    heads = gst_o.shape[1]
    keep = keep_column(sc, i * rows, rows)
    residual = res[...]
    lay_o[...] = (residual + keep * (fo[...] + dbias[...])).astype(bf16)
    scaled, inverse = standardize(residual)
    incoming = fig[...]
    cot_wide = cot[...].astype(f32)
    dbg = jnp.sum(keep * cot_wide, 0, keepdims=True)
    gg = jnp.sum(incoming * scaled, 0, keepdims=True)
    sg = jnp.sum(incoming, 0, keepdims=True)
    rg = cot_wide + norm_back(incoming, scaled, inverse, gain[...])
    rg_o[...] = rg
    ag = (keep * rg).astype(bf16)
    smalls = jnp.concatenate([dbg, gg, sg, jnp.zeros((5, dbg.shape[1]), f32)], 0)
    lanes = lane_ids(rows)

    @pl.when(i == 0)
    def _():
        small_o[...] = smalls
        og_o[...] = jnp.zeros_like(og_o)

    @pl.when(i > 0)
    def _():
        small_o[...] = small_o[...] + smalls

    for h in range(heads):
        hl = slice(h * LANES, (h + 1) * LANES)
        mg = nt(ag, wout[hl])
        numer = num[:, hl]
        inv = 1.0 / numer[:, 64:65]
        dg = -jnp.sum(jnp.where(lanes < 64, mg * numer, 0.0), -1, keepdims=True) * (inv * inv)
        ngx = jnp.where(lanes == 64, dg, mg * inv).astype(bf16)
        ngx_o[:, hl] = ngx
        gst_o[0, h] = tn(ngx, qf[:, h * TILE : (h + 1) * TILE])[:SROWS]
        og_o[h * 64 : (h + 1) * 64] += tn(mix[:, hl], ag)[:64]


def inner_kernel(q, qf, kf, vx, ngx, low, fo, qg_o, kn_o, vn_o):
    rows = q.shape[0]
    factor = 64 ** (-0.25)
    for base in range(0, rows, BLOCK):
        end = base + BLOCK
        for k in range(base, end, TILE):
            span = end - k
            row, column = causal_mask(TILE, span)
            ok = row <= column
            ks = slice(k, k + TILE)
            ts = slice(k, end)
            for h in range(2):
                fl = slice(h * TILE, (h + 1) * TILE)
                vl = slice(h * LANES, (h + 1) * LANES)
                scores = jnp.where(ok, nt(kf[ks, fl], qf[ts, fl]), 0.0).astype(bf16)
                vn_o[ks, vl] = nn(scores, ngx[ts, vl])
                grad = jnp.where(ok, nt(vx[ks, vl], ngx[ts, vl]), 0.0).astype(bf16)
                kn_o[ks, fl] = nn(grad, qf[ts, fl])
        for t in range(base, end, TILE):
            span = t + TILE - base
            row, column = causal_mask(TILE, span)
            ok = row + (t - base) >= column
            ts = slice(t, t + TILE)
            raws = []
            for h in range(2):
                fl = slice(h * TILE, (h + 1) * TILE)
                vl = slice(h * LANES, (h + 1) * LANES)
                ng = ngx[ts, vl]
                grad = jnp.where(ok, nt(ng, vx[base : base + span, vl]), 0.0).astype(bf16)
                qg = nn(grad, kf[base : base + span, fl]) + nn(ng, low[base // BLOCK, h])
                e = qg.astype(bf16).astype(f32) * qf[ts, fl].astype(f32)
                raws.append((factor * e).astype(bf16))
            raw = jnp.concatenate(raws, 1)
            qg_o[ts] = pair_back(raw, q[ts], fo[0]).astype(bf16)


def outer_kernel(sc, k, kf, vx, kn, vn, aft, gst, fo, kg_o, vg_o):
    rows = k.shape[0]
    blocks = rows // BLOCK
    factor = 64 ** (-0.25)
    pad = jnp.zeros((LANES - SROWS, TILE), f32)
    laters = []
    for h in range(2):
        state = aft[h]
        mine = [None] * blocks
        for b in range(blocks - 1, -1, -1):
            mine[b] = jnp.concatenate([state, pad], 0).astype(bf16)
            state = state + gst[b, h]
        laters.append(mine)
    for t in range(0, rows, TILE):
        ts = slice(t, t + TILE)
        keep = keep_column(sc, t, TILE)
        raws, vals = [], []
        for h in range(2):
            fl = slice(h * TILE, (h + 1) * TILE)
            vl = slice(h * LANES, (h + 1) * LANES)
            later = laters[h][t // BLOCK]
            keys = kf[ts, fl]
            kg = ((kn[ts, fl] + nn(vx[ts, vl], later)) * keep).astype(bf16)
            e = kg.astype(f32) * keys.astype(f32)
            raws.append((factor * e).astype(bf16))
            vals.append(vn[ts, vl] + nt(keys, later))
        kg_o[ts] = pair_back(jnp.concatenate(raws, 1), k[ts], fo[0]).astype(bf16)
        vg_o[ts] = join_pair(vals[0], vals[1]).astype(bf16)


def last_kernel(sc, tok, attn, rg, qg, kg, vg, win, gain, og, small, ubg, tok_o, keep_o, send_o):
    rows, width = tok.shape
    half = width // 2
    gg = jnp.zeros((1, width), f32)
    sg = jnp.zeros((1, width), f32)
    for t in range(0, rows, TILE):
        ts = slice(t, t + TILE)
        incoming = (
            nt(qg[ts], win[:, :width])
            + nt(kg[ts], win[:, width : 2 * width])
            + nt(vg[ts], win[:, 2 * width :])
        )
        scaled, inverse = standardize(tok[ts].astype(f32))
        gg = gg + jnp.sum(incoming * scaled, 0, keepdims=True)
        sg = sg + jnp.sum(incoming, 0, keepdims=True)
        tok_o[ts] = (rg[ts] + norm_back(incoming, scaled, inverse, gain[...])).astype(bf16)
    core = sc[2]
    base = 4 * width
    for ref, which in ((send_o, 1 - core), (keep_o, core)):
        first = pl.multiple_of(which * half, half)
        columns = attn[:, pl.ds(first, half)]
        ref[:, :width] = tn(columns, qg[...])
        ref[:, width : 2 * width] = tn(columns, kg[...])
        ref[:, 2 * width : 3 * width] = tn(columns, vg[...])
        ref[:, 3 * width : base] = og[pl.ds(first, half)]
        ref[:, base:] = jnp.zeros((half, LANES), f32)
        on = jnp.where(which == 0, 1.0, 0.0)
        row = 0
        vectors = [ubg[:, n : n + LANES] for n in range(0, ubg.shape[1], LANES)]
        for vec in (small[0:1], gg, sg, small[1:2], small[2:3]):
            vectors += [vec[:, n : n + LANES] for n in range(0, width, LANES)]
        for vec in vectors:
            ref[row : row + 1, base:] = vec * on
            row += 1


def call(kernel, outs, ins, args, grid=None, scratch=(), flops=0, limit=56):
    params = dict(vmem_limit_bytes=limit * 1024 * 1024)
    bytes_moved = sum(a.size * a.dtype.itemsize for a in args) + sum(
        s.size * s.dtype.itemsize for s, _ in outs
    )
    extra = {} if grid is None else {"grid": grid}
    return pl.pallas_call(
        kernel,
        out_shape=[s for s, _ in outs],
        in_specs=ins,
        out_specs=[s for _, s in outs],
        scratch_shapes=list(scratch),
        compiler_params=pltpu.CompilerParams(**params),
        cost_estimate=pl.CostEstimate(flops=int(flops), bytes_accessed=bytes_moved, transcendentals=0),
        **extra,
    )(*args)


def shape(dims, dtype):
    return jax.ShapeDtypeStruct(dims, dtype)


class Topology:
    def __init__(self, dp, seq):
        self.dp, self.seq = dp, seq
        self.core = 2
        self.x = seq // 2
        self.y = self.x if dp % self.x == 0 else 1
        self.z = dp // self.y
        self.size = {"c": self.core, "x": self.x, "y": self.y, "z": self.z}

    def split(self, flat):
        dp, seq = divmod(flat, self.seq)
        return {"z": dp // self.y, "y": dp % self.y, "x": seq // 2, "c": seq % 2}

    def flat(self, at):
        return (at["z"] * self.y + at["y"]) * self.seq + at["x"] * 2 + at["c"]

    def axis(self, step, core):
        if step == "1":
            return "xy"[core]
        if step == "2":
            return "yx"[core]
        return step

    def steps(self, step):
        return self.size[self.axis(step, 0)]

    def turn(self, step, by):
        pairs = []
        for source in range(self.dp * self.seq):
            at = self.split(source)
            name = self.axis(step, at["c"])
            at[name] = (at[name] + by) % self.size[name]
            pairs.append((source, self.flat(at)))
        return pairs

    def shift(self, dx, dc):
        pairs = []
        for source in range(self.dp * self.seq):
            at = self.split(source)
            at["x"], at["c"] = at["x"] + dx, at["c"] + dc
            if 0 <= at["x"] < self.x and 0 <= at["c"] < 2:
                pairs.append((source, self.flat(at)))
        return pairs

    def index(self, step):
        dp, seq = lax.axis_index("dp"), lax.axis_index("seq")
        here = {"z": dp // self.y, "y": dp % self.y, "x": seq // 2, "c": seq % 2}
        if step in "12":
            return jnp.where(
                here["c"] == 0, here[self.axis(step, 0)], here[self.axis(step, 1)]
            )
        return here[step]


def send(value, pairs):
    return lax.ppermute(value, AXES, pairs)


def scatter_step(topo, step, value):
    count, me = topo.steps(step), topo.index(step)
    rows = value.shape[0] // count
    part = lambda j: lax.dynamic_slice_in_dim(value, j * rows, rows, 0)
    got = [send(part((me + k) % count), topo.turn(step, k)) for k in range(1, count)]
    total = part(me)
    for piece in got:
        total = total + piece
    return total


def gather_step(topo, step, value):
    count, me = topo.steps(step), topo.index(step)
    rows = value.shape[0]
    got = [value] + [send(value, topo.turn(step, k)) for k in range(1, count)]
    if count == 2:
        return jnp.where(
            me == 0, jnp.concatenate(got, 0), jnp.concatenate(got[::-1], 0)
        )
    out = jnp.zeros((count * rows,) + value.shape[1:], value.dtype)
    for k in range(count):
        out = lax.dynamic_update_slice_in_dim(out, got[k], ((me - k) % count) * rows, 0)
    return out


def reduce_all(topo, mine, other):
    total = mine + send(other, topo.turn("c", 1))
    for step in "12z":
        total = scatter_step(topo, step, total)
    for step in "z21c":
        total = gather_step(topo, step, total)
    return total


def sums_before(topo, mine):
    near = send(mine, topo.turn("c", 1))
    chip = mine + near
    total = jnp.where(topo.index("c") == 1, near, 0.0)
    for k in range(1, topo.x):
        total = total + send(chip, topo.shift(k, 0))
    return total


def sums_after(topo, mine):
    near = send(mine, topo.turn("c", 1))
    chip = mine + near
    total = jnp.where(topo.index("c") == 0, near, 0.0)
    for k in range(1, topo.x):
        total = total + send(chip, topo.shift(-k, 0))
    return total


def build(topo):
    def local(tokens, in_proj, out_proj, up_proj, down_proj, up_bias, down_bias, attn_gain,
              attn_shift, ffn_gain, ffn_shift, feature_matrix, lengths, slot_of_seq, cotangent):
        rows, width = tokens.shape[1:]
        heads, size, feats = feature_matrix.shape
        pairs = heads // 2
        ff = up_proj.shape[1]
        blocks = rows // BLOCK
        tok, cot = tokens[0], cotangent[0]
        seq_len = jnp.sum(lengths * (slot_of_seq == lax.axis_index("dp")).astype(jnp.int32))
        sc = jnp.stack([lax.axis_index("seq") * rows, seq_len, topo.index("c"), 0]).astype(jnp.int32)
        vec = lambda v: v.astype(f32)[None]
        zero = jnp.zeros((pairs, size, feats), bf16)
        one = jnp.ones((pairs, size, feats), bf16)
        fpair = feature_matrix.reshape(pairs, 2, size, feats)
        block_of = lambda a, b: jnp.concatenate(
            [jnp.concatenate([a, zero], 2), jnp.concatenate([zero, b], 2)], 1
        )
        fo = jnp.concatenate([block_of(fpair[:, 0], fpair[:, 1]), block_of(one, one)], 1)
        wout = jnp.pad(out_proj.reshape(heads, size, width), ((0, 0), (0, LANES - size), (0, 0)))
        wout = wout.reshape(heads * LANES, width)

        smem = pl.BlockSpec(memory_space=pltpu.SMEM)
        ext = heads * LANES
        fw = heads * feats
        row_spec = lambda w: pl.BlockSpec((BLOCK, w), lambda i: (i, 0))
        whole = lambda *dims: pl.BlockSpec(dims, lambda i: (0,) * len(dims))
        pair_col = lambda w: pl.BlockSpec((rows, w), lambda p: (0, p))

        attn_in, k, vx, kf, st = call(
            key_kernel,
            [
                (shape((rows, width), bf16), row_spec(width)),
                (shape((rows, width), bf16), row_spec(width)),
                (shape((rows, ext), bf16), row_spec(ext)),
                (shape((rows, fw), bf16), row_spec(fw)),
                (shape((blocks, heads, SROWS, feats), f32),
                 pl.BlockSpec((1, heads, SROWS, feats), lambda i: (i, 0, 0, 0))),
            ],
            [smem, row_spec(width), whole(width, 2 * width), whole(1, width), whole(1, width),
             whole(pairs, 2 * LANES, 2 * feats)],
            [sc, tok, in_proj[:, width:], vec(attn_gain), vec(attn_shift), fo],
            grid=(blocks,),
            flops=5e9,
        )
        prefix = sums_before(topo, jnp.sum(st, 0).reshape(heads * SROWS, feats))
        prefix = prefix.reshape(heads, SROWS, feats)
        q, qf, near = call(
            near_kernel,
            [
                (shape((rows, width), bf16), pair_col(LANES)),
                (shape((rows, fw), bf16), pair_col(2 * feats)),
                (shape((rows, ext), f32), pair_col(2 * LANES)),
            ],
            [whole(rows, width), pl.BlockSpec((width, LANES), lambda p: (0, p)),
             pl.BlockSpec((1, 2 * LANES, 2 * feats), lambda p: (p, 0, 0)),
             pair_col(2 * feats), pair_col(2 * LANES)],
            [attn_in, in_proj, fo, kf, vx],
            grid=(pairs,),
            flops=7e9,
        )
        num, mix, low, res, fin = call(
            mix_kernel,
            [
                (shape((rows, ext), f32), row_spec(ext)),
                (shape((rows, ext), bf16), row_spec(ext)),
                (shape((blocks, heads, LANES, feats), bf16),
                 pl.BlockSpec((1, heads, LANES, feats), lambda i: (i, 0, 0, 0))),
                (shape((rows, width), f32), row_spec(width)),
                (shape((rows, width), bf16), row_spec(width)),
            ],
            [smem, row_spec(ext), row_spec(fw), whole(heads, SROWS, feats),
             whole(blocks, heads, SROWS, feats), row_spec(width), whole(ext, width),
             whole(1, width), whole(1, width)],
            [sc, near, qf, prefix, st, tok, wout, vec(ffn_gain), vec(ffn_shift)],
            grid=(blocks,),
            flops=3e9,
        )

        chunk = 512
        halves = 2
        per = ff // chunk // halves

        def ffn(half, carried):
            outs = [
                (shape((width // 2, 4 * chunk), f32), whole(width // 2, 4 * chunk)),
                (shape((width // 2, 4 * chunk), f32), whole(width // 2, 4 * chunk)),
                (shape((rows, width), f32), whole(rows, width)),
                (shape((rows, width), f32), whole(rows, width)),
                (shape((1, per * chunk), f32), pl.BlockSpec((1, chunk), lambda j: (0, j))),
            ]
            ins = [smem, whole(rows, width), whole(rows, width),
                   pl.BlockSpec((width, chunk), lambda j: (0, half * per + j)),
                   pl.BlockSpec((chunk, width), lambda j: (half * per + j, 0)),
                   pl.BlockSpec((1, chunk), lambda j: (0, half * per + j))]
            ins += [whole(rows, width)] * len(carried)
            return call(
                ffn_second if carried else ffn_first, outs, ins,
                [sc, fin, cot, up_proj, down_proj, vec(up_bias)] + carried,
                grid=(per,),
                scratch=[pltpu.VMEM((rows, width), bf16), pltpu.VMEM((rows, chunk), bf16),
                         pltpu.VMEM((rows, chunk), bf16)],
                flops=7e9,
            )

        mine0, other0, fo0, fig0, ubg0 = ffn(0, [])
        mine1, other1, ffn_out, fig, ubg1 = ffn(1, [fo0, fig0])
        sum0 = reduce_all(topo, mine0, other0)
        sum1 = reduce_all(topo, mine1, other1)

        lay, rg, ngx, gst, og, small = call(
            middle_kernel,
            [
                (shape((rows, width), bf16), row_spec(width)),
                (shape((rows, width), f32), row_spec(width)),
                (shape((rows, ext), bf16), row_spec(ext)),
                (shape((blocks, heads, SROWS, feats), f32),
                 pl.BlockSpec((1, heads, SROWS, feats), lambda i: (i, 0, 0, 0))),
                (shape((width, width), f32), whole(width, width)),
                (shape((8, width), f32), whole(8, width)),
            ],
            [smem, row_spec(width), row_spec(width), row_spec(width), row_spec(width),
             row_spec(ext), row_spec(ext), row_spec(fw), whole(ext, width), whole(1, width),
             whole(1, width)],
            [sc, ffn_out, fig, res, cot, mix, num, qf, wout, vec(ffn_gain), vec(down_bias)],
            grid=(blocks,),
            flops=5e9,
        )
        after = sums_after(topo, jnp.sum(gst, 0).reshape(heads * SROWS, feats))
        after = after.reshape(heads, SROWS, feats)
        fo_pair = pl.BlockSpec((1, 2 * LANES, 2 * feats), lambda p: (p, 0, 0))
        low_pair = pl.BlockSpec((blocks, 2, LANES, feats), lambda p: (0, p, 0, 0))
        gst_pair = pl.BlockSpec((blocks, 2, SROWS, feats), lambda p: (0, p, 0, 0))
        qg, kn, vn = call(
            inner_kernel,
            [
                (shape((rows, width), bf16), pair_col(LANES)),
                (shape((rows, fw), f32), pair_col(2 * feats)),
                (shape((rows, ext), f32), pair_col(2 * LANES)),
            ],
            [pair_col(LANES), pair_col(2 * feats), pair_col(2 * feats), pair_col(2 * LANES),
             pair_col(2 * LANES), low_pair, fo_pair],
            [q, qf, kf, vx, ngx, low, fo],
            grid=(pairs,),
            flops=14e9,
        )
        kg, vg = call(
            outer_kernel,
            [
                (shape((rows, width), bf16), pair_col(LANES)),
                (shape((rows, width), bf16), pair_col(LANES)),
            ],
            [smem, pair_col(LANES), pair_col(2 * feats), pair_col(2 * LANES), pair_col(2 * feats),
             pair_col(2 * LANES), pl.BlockSpec((2, SROWS, feats), lambda p: (p, 0, 0)), gst_pair,
             fo_pair],
            [sc, k, kf, vx, kn, vn, after, gst, fo],
            grid=(pairs,),
            flops=5e9,
        )
        vmem = pl.BlockSpec(memory_space=pltpu.VMEM)
        grad_tok, mine2, other2 = call(
            last_kernel,
            [
                (shape((rows, width), bf16), vmem),
                (shape((width // 2, 4 * width + LANES), f32), vmem),
                (shape((width // 2, 4 * width + LANES), f32), vmem),
            ],
            [smem] + [vmem] * 11,
            [sc, tok, attn_in, rg, qg, kg, vg, in_proj, vec(attn_gain), og, small,
             jnp.concatenate([ubg0, ubg1], 1)],
            flops=6e9,
        )
        sum2 = reduce_all(topo, mine2, other2)

        hid = per * chunk
        grad_up = jnp.concatenate([sum0[:, :hid], sum1[:, :hid]], 1)
        grad_down = jnp.concatenate(
            [s[:, hid + n * width : hid + (n + 1) * width] for s in (sum0, sum1) for n in range(per)], 0
        )
        tail = sum2[: (ff + 5 * width) // LANES, 4 * width :].reshape(-1)
        cut = lambda n: tail[ff + n * width : ff + (n + 1) * width]
        return (
            lay[None], grad_tok[None], sum2[:, : 3 * width], sum2[:, 3 * width : 4 * width],
            grad_up, grad_down, tail[:ff], cut(0), cut(1), cut(2), cut(3), cut(4),
        )

    return local


def solution(mesh):
    rowwise = P("dp", "seq", None)
    return jax.shard_map(
        build(Topology(mesh.shape["dp"], mesh.shape["seq"])),
        mesh=mesh,
        in_specs=(rowwise,) + (P(),) * 13 + (rowwise,),
        out_specs=(rowwise, rowwise) + (P(),) * 10,
        check_vma=False,
    )
```
